512 devices in a mesh: ctx: 32 (over x_lo, z), fsdp: 16 (over x_hi, y, core).
Axes of the slice: x: 4 (x_hi: 2, x_lo: 2; x = x_hi * 2 + x_lo), y: 4, z: 16, core: 2. Of those that a mesh axis runs over, the one named last changes fastest.
Arguments:
- streams: bfloat16 [16, 4096, 12288], P('fsdp', 'ctx'), may hold values from -18 to 18
- filters: float32 [3, 3, 4096], P(None, None, 'fsdp'), may hold values from 0.1 to 1.9
Outputs:
- attended: bfloat16 [16, 4096, 4096], P('fsdp', 'ctx')
The draws below stay inside these ranges and needn't reach their ends.
All inputs are finite; a program needn't handle non-finite values.
Results may differ from the reference program's by a relative error of at most 0.011.
Values may be sent and summed in bfloat16 or wider, within the bound.
No kernel may reach another device: no remote copies, remote signals or barrier semaphores. Data moves between devices by JAX's collectives and lax.ppermute only.
A program may use at most 64 MiB of HBM per device.

```python
import jax
import jax.numpy as jnp
from jax import lax

HEADS = 32
HEAD_DIM = 128
TAPS = 3
SEQS = 16
LENGTH = 4096
CHANNELS = 4096


def draw_streams(key, part):
    key = jax.random.fold_in(key, 7)
    full_shape = (SEQS, LENGTH, 3, HEADS, HEAD_DIM)
    values_all = jnp.clip(jax.random.normal(key, full_shape, jnp.float32), -6.0, 6.0)
    return values_all.reshape(SEQS, LENGTH, 3 * HEADS * HEAD_DIM).astype(jnp.bfloat16)


def setup_inputs(seed: int = 0) -> dict:
    streams_of = jax.random.split(jax.random.key(seed), 3)
    return {
        "streams": draw_streams(jax.random.fold_in(streams_of[2], 71), 0),
        "filters": jnp.clip(1.0 + 0.18 * jax.random.normal(streams_of[1], (3, TAPS, CHANNELS), jnp.float32), 0.1, 1.9),
    }


def featurize(streams_all, filters):
    seq_count, length_all, channel_width = streams_all.shape
    grouped = streams_all.reshape(seq_count, length_all, 3, HEADS, HEAD_DIM).astype(jnp.float32)
    tap_table = filters.reshape(3, TAPS, HEADS, HEAD_DIM)
    padded = jnp.pad(grouped, ((0, 0), (TAPS - 1, 0), (0, 0), (0, 0), (0, 0)))
    summed = jnp.zeros(grouped.shape, jnp.float32)
    for offset in range(TAPS):
        summed = summed + tap_table[:, offset] * padded[:, TAPS - 1 - offset:TAPS - 1 - offset + length_all]
    return summed.astype(jnp.bfloat16)


def attend_one(sequence):
    length_all = sequence.shape[0]
    block_rows = length_all if length_all <= 512 else max(512, length_all // 8)
    queries = sequence[:, 0].astype(jnp.float32)
    keys_all = sequence[:, 1].astype(jnp.float32)
    values_all = sequence[:, 2].astype(jnp.float32)
    scale_factor = sequence.shape[-1] ** -0.5
    pieces = []
    for number in range(length_all // block_rows):
        first = number * block_rows
        final = first + block_rows
        scores = jnp.einsum("qhe,khe->hqk", queries[first:final], keys_all[:final]) * scale_factor
        query_pos = first + jnp.arange(block_rows)
        key_pos = jnp.arange(final)
        scores = jnp.where(key_pos[None, None, :] <= query_pos[None, :, None], scores, -jnp.inf)
        highest = jnp.max(scores, axis=-1, keepdims=True)
        exponent = jnp.exp(scores - highest)
        totals = jnp.sum(exponent, axis=-1)
        weights = exponent.astype(jnp.bfloat16)
        summed = jnp.einsum("hqk,khe->qhe", weights.astype(jnp.float32), values_all[:final])
        pieces.append((summed / totals.T[:, :, None]).astype(jnp.bfloat16))
    return jnp.concatenate(pieces, axis=0)


def reference(streams, filters):
    featured = featurize(streams, filters)
    attended = lax.map(attend_one, featured)
    return attended.reshape(SEQS, LENGTH, CHANNELS)
```

```python
import functools
import math

import jax
import jax.numpy as jnp
from jax import lax
from jax.experimental import pallas as pl
from jax.experimental.pallas import tpu as pltpu
from jax.sharding import PartitionSpec as P

HEADS = 32
HEAD_DIM = 128
TAPS = 3
SCALE = HEAD_DIM**-0.5 * math.log2(math.e)


def featurize_into(x_ref, column, taps_ref, stream, store):
    length = x_ref.shape[0]
    rows = 256
    taps = [taps_ref[stream, offset : offset + 1, :] for offset in range(TAPS)]

    def step(number, rim):
        first = pl.multiple_of(number * rows, rows)
        x = x_ref[pl.ds(first, rows), column : column + HEAD_DIM].astype(jnp.float32)
        extended = jnp.concatenate([rim, x], axis=0)
        summed = taps[0] * x + taps[1] * extended[7 : 7 + rows] + taps[2] * extended[6 : 6 + rows]
        store(first, rows, summed)
        return x[rows - 8 :]

    lax.fori_loop(0, length // rows, step, jnp.zeros((8, HEAD_DIM), jnp.float32))


def attention_kernel(bq, bk, x_ref, taps_ref, o_ref, qf, kf, vt, held, acc):
    length = x_ref.shape[0]

    def store_q(first, rows, summed):
        qf[pl.ds(first, rows), :] = summed.astype(jnp.bfloat16)

    def store_k(first, rows, summed):
        kf[pl.ds(first, rows), :] = summed.astype(jnp.bfloat16)

    def store_v(first, rows, summed):
        vt[:, pl.ds(first, rows)] = summed.T.astype(jnp.bfloat16)

    featurize_into(x_ref, 0, taps_ref, 0, store_q)
    featurize_into(x_ref, HEAD_DIM, taps_ref, 1, store_k)
    featurize_into(x_ref, 2 * HEAD_DIM, taps_ref, 2, store_v)

    def scores(q, j):
        k = kf[pl.ds(pl.multiple_of(j * bk, bk), bk), :]
        return lax.dot_general(k, q, (((1,), (1,)), ((), ())), preferred_element_type=jnp.float32)

    def process(s, j, m, l):
        new = jnp.maximum(m, jnp.max(s, axis=0, keepdims=True))
        alpha = jnp.exp2((m - new) * SCALE)
        p = jnp.exp2((s - new) * SCALE)
        l = l * alpha + jnp.sum(p, axis=0, keepdims=True)
        v = vt[:, pl.ds(pl.multiple_of(j * bk, bk), bk)]
        acc[...] = acc[...] * alpha + jnp.dot(
            v, p.astype(jnp.bfloat16), preferred_element_type=jnp.float32
        )
        return new, l

    def q_block(i, _):
        first = pl.multiple_of(i * bq, bq)
        q = qf[pl.ds(first, bq), :]
        acc[...] = jnp.zeros_like(acc)
        full = (i * bq) // bk
        held[0] = scores(q, 0)

        def body(j, ml):
            slot = lax.rem(j, 2)
            held[1 - slot] = scores(q, j + 1)
            return process(held[slot], j, *ml)

        start = (jnp.full((1, bq), -jnp.inf, jnp.float32), jnp.zeros((1, bq), jnp.float32))
        m, l = lax.fori_loop(0, full, body, start)
        key_pos = full * bk + lax.broadcasted_iota(jnp.int32, (bk, bq), 0)
        query_pos = i * bq + lax.broadcasted_iota(jnp.int32, (bk, bq), 1)
        s = jnp.where(key_pos <= query_pos, held[lax.rem(full, 2)], -jnp.inf)
        m, l = process(s, full, m, l)
        o_ref[pl.ds(first, bq), :] = (acc[...] / l).T.astype(jnp.bfloat16)
        return 0

    lax.fori_loop(0, length // bq, q_block, 0)


def attend(x, taps, bq=1024, bk=1024):
    length = x.shape[0]
    return pl.pallas_call(
        functools.partial(attention_kernel, bq, bk),
        out_shape=jax.ShapeDtypeStruct((length, HEAD_DIM), jnp.bfloat16),
        in_specs=[pl.BlockSpec(memory_space=pltpu.VMEM)] * 2,
        out_specs=pl.BlockSpec(memory_space=pltpu.VMEM),
        scratch_shapes=[
            pltpu.VMEM((length, HEAD_DIM), jnp.bfloat16),
            pltpu.VMEM((length, HEAD_DIM), jnp.bfloat16),
            pltpu.VMEM((HEAD_DIM, length), jnp.bfloat16),
            pltpu.VMEM((2, bk, bq), jnp.float32),
            pltpu.VMEM((HEAD_DIM, bq), jnp.float32),
        ],
        compiler_params=pltpu.CompilerParams(vmem_limit_bytes=44 * 2**20),
        name="attention",
    )(x, taps)


def own_taps(filters):
    head = lax.axis_index("ctx")
    here = filters.shape[2] // HEAD_DIM
    mine = lax.dynamic_slice_in_dim(filters, (head % here) * HEAD_DIM, HEAD_DIM, axis=2)
    mine = jnp.where(head // here == lax.axis_index("fsdp"), mine, 0.0)
    return lax.psum(mine, "fsdp")


def on_device(streams, filters):
    seqs_here, positions, channel_width = streams.shape
    taps = own_taps(filters)
    by_head = streams.reshape(positions, 3, HEADS, HEAD_DIM).transpose(2, 0, 1, 3)
    by_head = by_head.reshape(HEADS, positions, 3 * HEAD_DIM)
    arrived = lax.all_to_all(by_head, "ctx", split_axis=0, concat_axis=0, tiled=True)
    attended = attend(arrived.reshape(HEADS * positions, 3 * HEAD_DIM), taps)
    outgoing = attended.reshape(HEADS, positions, HEAD_DIM)
    returned = lax.all_to_all(outgoing, "ctx", split_axis=0, concat_axis=0, tiled=True)
    return returned.transpose(1, 0, 2).reshape(seqs_here, positions, HEADS * HEAD_DIM)


def solution(mesh):
    placed = (P("fsdp", "ctx", None), P(None, None, "fsdp"))
    return jax.shard_map(
        on_device, mesh=mesh, in_specs=placed, out_specs=P("fsdp", "ctx", None), check_vma=False
    )
```

```python
import functools
import math

import jax
import jax.numpy as jnp
from jax import lax
from jax.experimental import pallas as pl
from jax.experimental.pallas import tpu as pltpu
from jax.sharding import PartitionSpec as P

HEADS = 32
HEAD_DIM = 128
TAPS = 3
SCALE = HEAD_DIM**-0.5 * math.log2(math.e)
TILE = 256
STRETCH = 1024
ROWS = 16
HEADS_AT_A_TIME = 8
HEADROOM = 60.0
VMEM = pl.BlockSpec(memory_space=pltpu.VMEM)


def split_kernel(x_ref, out_ref, rows, by_head, arrived, sent):
    positions, width = x_ref.shape
    step = HEADS_AT_A_TIME * HEAD_DIM

    def fetch(part):
        columns = pl.ds(part * step, step)
        return pltpu.make_async_copy(x_ref.at[:, columns], rows.at[:, columns], arrived.at[part])

    def send(part):
        stream, first = divmod(part * HEADS_AT_A_TIME, HEADS)
        heads, kept = pl.ds(first, HEADS_AT_A_TIME), pl.ds(stream * positions, positions)
        place = out_ref.at[heads, kept, :]
        return pltpu.make_async_copy(by_head.at[heads, kept, :], place, sent.at[part])

    for part in range(width // step):
        fetch(part).start()
    for part in range(width // step):
        fetch(part).wait()
        for column in range(part * HEADS_AT_A_TIME, (part + 1) * HEADS_AT_A_TIME):
            stream, head = divmod(column, HEADS)
            by_head[head, stream * positions : (stream + 1) * positions, :] = rows[
                :, column * HEAD_DIM : (column + 1) * HEAD_DIM
            ]
        send(part).start()
    for part in range(width // step):
        send(part).wait()


def split_by_head(streams):
    positions, width = streams.shape
    parts = 3 * HEADS // HEADS_AT_A_TIME
    shape = (HEADS, 3 * positions, HEAD_DIM)
    return pl.pallas_call(
        split_kernel,
        out_shape=jax.ShapeDtypeStruct(shape, jnp.bfloat16),
        in_specs=[pl.BlockSpec(memory_space=pltpu.HBM)],
        out_specs=pl.BlockSpec(memory_space=pltpu.HBM),
        scratch_shapes=[
            pltpu.VMEM((positions, width), jnp.bfloat16),
            pltpu.VMEM(shape, jnp.bfloat16),
            pltpu.SemaphoreType.DMA((parts,)),
            pltpu.SemaphoreType.DMA((parts,)),
        ],
        compiler_params=pltpu.CompilerParams(vmem_limit_bytes=58 * 2**20),
        name="split_by_head",
    )(streams)


def merge_kernel(in_ref, out_ref, rows, sent):
    heads, positions, _ = in_ref.shape
    count = positions // ROWS

    def copy(part):
        chunk = pl.ds(part * ROWS, ROWS)
        return pltpu.make_async_copy(rows.at[chunk, :], out_ref.at[chunk, :], sent.at[part])

    for part in range(count):
        first = part * ROWS
        for head in range(heads):
            rows[first : first + ROWS, head * HEAD_DIM : (head + 1) * HEAD_DIM] = in_ref[
                head, first : first + ROWS, :
            ]
        copy(part).start()
    for part in range(count):
        copy(part).wait()


def merge_heads(parts):
    heads, positions, _ = parts.shape
    return pl.pallas_call(
        merge_kernel,
        out_shape=jax.ShapeDtypeStruct((positions, heads * HEAD_DIM), jnp.bfloat16),
        in_specs=[VMEM],
        out_specs=pl.BlockSpec(memory_space=pltpu.HBM),
        scratch_shapes=[
            pltpu.VMEM((positions, heads * HEAD_DIM), jnp.bfloat16),
            pltpu.SemaphoreType.DMA((positions // ROWS,)),
        ],
        compiler_params=pltpu.CompilerParams(vmem_limit_bytes=16 * 2**20),
        name="merge_heads",
    )(parts)


def sublanes(x):
    return x.reshape(x.shape[0] // 8, 8, x.shape[1])


def attention_kernel(x_ref, taps_ref, o_ref, qt, kf, vt, held, *weights):
    shards, positions = x_ref.shape[0], x_ref.shape[1] // 3
    length = shards * positions
    taps = [[taps_ref[s, offset : offset + 1, :] for offset in range(TAPS)] for s in range(3)]

    def featurize(first, rows):
        for s in range(3):
            shard, after = first // positions, (first + rows) // positions
            x = x_ref[shard:after, s * positions : (s + 1) * positions, :]
            x = x.reshape(rows, HEAD_DIM).astype(jnp.float32)
            held[s, 8 + first : 8 + first + rows] = x
            summed = taps[s][0] * x
            for offset in range(1, TAPS):
                start = 8 - offset + first
                summed = summed + taps[s][offset] * held[s, start : start + rows]
            featured = summed.astype(jnp.bfloat16)
            if s == 1:
                kf[first : first + rows, :] = featured
            else:
                (qt if s == 0 else vt)[:, first : first + rows] = featured.T

    def scores(key, q):
        return jnp.dot(kf[pl.ds(key, TILE), :], q, preferred_element_type=jnp.float32)

    down = lax.broadcasted_iota(jnp.int32, (TILE, TILE), 0)
    across = lax.broadcasted_iota(jnp.int32, (TILE, TILE), 1)

    def attend(t):
        first, end = t * TILE, (t + 1) * TILE
        rounded = weights[t % len(weights)]
        q = qt[:, first:end]
        s = sublanes(jnp.where(down <= across, scores(first, q), -jnp.inf))
        shift = jnp.max(s, axis=0)
        shift = jnp.broadcast_to(jnp.max(shift, axis=0, keepdims=True), shift.shape)
        exponent = jnp.exp2((s - shift) * SCALE)
        total, highest = jnp.sum(exponent, axis=0), shift
        rounded[first:end] = exponent.reshape(TILE, TILE).astype(jnp.bfloat16)
        for key in range(0, first, TILE):
            s = sublanes(scores(key, q))
            highest = jnp.maximum(highest, jnp.max(s, axis=0))
            exponent = jnp.exp2((s - shift) * SCALE)
            total = total + jnp.sum(exponent, axis=0)
            rounded[key : key + TILE] = exponent.reshape(TILE, TILE).astype(jnp.bfloat16)
        summed = jnp.dot(vt[:, :end], rounded[:end], preferred_element_type=jnp.float32)
        attended = summed / jnp.sum(total, axis=0, keepdims=True)
        o_ref[first:end, :] = attended.T.astype(jnp.bfloat16)
        return jnp.max(highest - shift)

    for s in range(3):
        held[s, :8] = jnp.zeros((8, HEAD_DIM), jnp.float32)
    above = 0.0
    for t in range(length // TILE):
        if (t * TILE) % STRETCH == 0:
            featurize(t * TILE, STRETCH)
        above = jnp.maximum(above, attend(t))

    @pl.when(above * SCALE > HEADROOM)
    def _():
        def query_tile(t, _):
            first = pl.multiple_of(t * TILE, TILE)
            q = qt[:, pl.ds(first, TILE)]

            def key_tile(number, carry):
                m, l, acc = carry
                key = pl.multiple_of(number * TILE, TILE)
                s = jnp.where(key + down <= first + across, scores(key, q), -jnp.inf)
                new = jnp.maximum(m, jnp.max(s, axis=0, keepdims=True))
                alpha = jnp.exp2((m - new) * SCALE)
                exponent = jnp.exp2((s - new) * SCALE)
                l = l * alpha + jnp.sum(exponent, axis=0, keepdims=True)
                acc = acc * alpha + jnp.dot(
                    vt[:, pl.ds(key, TILE)],
                    exponent.astype(jnp.bfloat16),
                    preferred_element_type=jnp.float32,
                )
                return new, l, acc

            start = (
                jnp.full((1, TILE), -jnp.inf, jnp.float32),
                jnp.zeros((1, TILE), jnp.float32),
                jnp.zeros((HEAD_DIM, TILE), jnp.float32),
            )
            _, l, acc = lax.fori_loop(0, t + 1, key_tile, start)
            o_ref[pl.ds(first, TILE), :] = (acc / l).T.astype(jnp.bfloat16)
            return 0

        lax.fori_loop(0, length // TILE, query_tile, 0)


def attention(x, taps):
    shards, rows, _ = x.shape
    length = shards * rows // 3
    return pl.pallas_call(
        attention_kernel,
        out_shape=jax.ShapeDtypeStruct((length, HEAD_DIM), jnp.bfloat16),
        in_specs=[VMEM] * 2,
        out_specs=VMEM,
        scratch_shapes=[
            pltpu.VMEM((HEAD_DIM, length), jnp.bfloat16),
            pltpu.VMEM((length, HEAD_DIM), jnp.bfloat16),
            pltpu.VMEM((HEAD_DIM, length), jnp.bfloat16),
            pltpu.VMEM((3, 8 + length, HEAD_DIM), jnp.float32),
            pltpu.VMEM((length, TILE), jnp.bfloat16),
            pltpu.VMEM((length, TILE), jnp.bfloat16),
        ],
        compiler_params=pltpu.CompilerParams(vmem_limit_bytes=32 * 2**20),
        name="attention",
    )(x, taps)


def own_taps(filters):
    head = lax.axis_index("ctx")
    here = filters.shape[2] // HEAD_DIM
    mine = lax.dynamic_slice_in_dim(filters, (head % here) * HEAD_DIM, HEAD_DIM, axis=2)
    mine = jnp.where(head // here == lax.axis_index("fsdp"), mine, 0.0)
    return lax.psum(mine, "fsdp")


def exchanged(parts):
    return lax.all_to_all(parts, "ctx", split_axis=0, concat_axis=0, tiled=True)


def on_device(streams, filters):
    seqs_here, positions, channel_width = streams.shape
    taps = own_taps(filters)
    arrived = exchanged(split_by_head(streams.reshape(positions, channel_width)))
    attended = attention(arrived, taps)
    returned = exchanged(attended.reshape(HEADS, positions, HEAD_DIM))
    return merge_heads(returned).reshape(seqs_here, positions, HEADS * HEAD_DIM)


def solution(mesh):
    placed = (P("fsdp", "ctx", None), P(None, None, "fsdp"))
    return jax.shard_map(
        on_device, mesh=mesh, in_specs=placed, out_specs=P("fsdp", "ctx", None), check_vma=False
    )
```

```python
import functools
import math

import jax
import jax.numpy as jnp
from jax import lax
from jax.experimental import pallas as pl
from jax.experimental.pallas import tpu as pltpu
from jax.sharding import PartitionSpec as P

HEADS = 32
HEAD_DIM = 128
TAPS = 3
SCALE = HEAD_DIM**-0.5 * math.log2(math.e)
TILE = 256
STRETCH = 1024
ROWS = 16
HEADS_AT_A_TIME = 8
HIGHEST_TOTAL = 2.0**60
VMEM = pl.BlockSpec(memory_space=pltpu.VMEM)


def split_kernel(x_ref, out_ref, rows, by_head, arrived, sent):
    positions, width = x_ref.shape
    step = HEADS_AT_A_TIME * HEAD_DIM

    def fetch(part):
        columns = pl.ds(part * step, step)
        return pltpu.make_async_copy(x_ref.at[:, columns], rows.at[:, columns], arrived.at[part])

    def send(part):
        stream, first = divmod(part * HEADS_AT_A_TIME, HEADS)
        heads, kept = pl.ds(first, HEADS_AT_A_TIME), pl.ds(stream * positions, positions)
        place = out_ref.at[heads, kept, :]
        return pltpu.make_async_copy(by_head.at[heads, kept, :], place, sent.at[part])

    for part in range(width // step):
        fetch(part).start()
    for part in range(width // step):
        fetch(part).wait()
        for column in range(part * HEADS_AT_A_TIME, (part + 1) * HEADS_AT_A_TIME):
            stream, head = divmod(column, HEADS)
            by_head[head, stream * positions : (stream + 1) * positions, :] = rows[
                :, column * HEAD_DIM : (column + 1) * HEAD_DIM
            ]
        send(part).start()
    for part in range(width // step):
        send(part).wait()


def split_by_head(streams):
    positions, width = streams.shape
    parts = 3 * HEADS // HEADS_AT_A_TIME
    shape = (HEADS, 3 * positions, HEAD_DIM)
    return pl.pallas_call(
        split_kernel,
        out_shape=jax.ShapeDtypeStruct(shape, jnp.bfloat16),
        in_specs=[pl.BlockSpec(memory_space=pltpu.HBM)],
        out_specs=pl.BlockSpec(memory_space=pltpu.HBM),
        scratch_shapes=[
            pltpu.VMEM((positions, width), jnp.bfloat16),
            pltpu.VMEM(shape, jnp.bfloat16),
            pltpu.SemaphoreType.DMA((parts,)),
            pltpu.SemaphoreType.DMA((parts,)),
        ],
        compiler_params=pltpu.CompilerParams(vmem_limit_bytes=58 * 2**20),
        name="split_by_head",
    )(streams)


def merge_kernel(in_ref, out_ref, rows, sent):
    heads, positions, _ = in_ref.shape
    count = positions // ROWS

    def copy(part):
        chunk = pl.ds(part * ROWS, ROWS)
        return pltpu.make_async_copy(rows.at[chunk, :], out_ref.at[chunk, :], sent.at[part])

    for part in range(count):
        first = part * ROWS
        for head in range(heads):
            rows[first : first + ROWS, head * HEAD_DIM : (head + 1) * HEAD_DIM] = in_ref[
                head, first : first + ROWS, :
            ]
        copy(part).start()
    for part in range(count):
        copy(part).wait()


def merge_heads(parts):
    heads, positions, _ = parts.shape
    return pl.pallas_call(
        merge_kernel,
        out_shape=jax.ShapeDtypeStruct((positions, heads * HEAD_DIM), jnp.bfloat16),
        in_specs=[VMEM],
        out_specs=pl.BlockSpec(memory_space=pltpu.HBM),
        scratch_shapes=[
            pltpu.VMEM((positions, heads * HEAD_DIM), jnp.bfloat16),
            pltpu.SemaphoreType.DMA((positions // ROWS,)),
        ],
        compiler_params=pltpu.CompilerParams(vmem_limit_bytes=16 * 2**20),
        name="merge_heads",
    )(parts)


def sublanes(x):
    return x.reshape(x.shape[0] // 8, 8, x.shape[1])


def attention_kernel(x_ref, taps_ref, o_ref, qt, kf, vt, held, *weights):
    shards, positions = x_ref.shape[0], x_ref.shape[1] // 3
    length = shards * positions
    taps = [[taps_ref[s, offset : offset + 1, :] for offset in range(TAPS)] for s in range(3)]

    def featurize(first, rows):
        for s in range(3):
            shard, after = first // positions, (first + rows) // positions
            x = x_ref[shard:after, s * positions : (s + 1) * positions, :]
            x = x.reshape(rows, HEAD_DIM).astype(jnp.float32)
            held[s, 8 + first : 8 + first + rows] = x
            summed = taps[s][0] * x
            for offset in range(1, TAPS):
                start = 8 - offset + first
                summed = summed + taps[s][offset] * held[s, start : start + rows]
            featured = summed.astype(jnp.bfloat16)
            if s == 1:
                kf[first : first + rows, :] = featured
            else:
                (qt if s == 0 else vt)[:, first : first + rows] = featured.T

    def scores(key, q):
        return jnp.dot(kf[pl.ds(key, TILE), :], q, preferred_element_type=jnp.float32)

    down = lax.broadcasted_iota(jnp.int32, (TILE, TILE), 0)
    across = lax.broadcasted_iota(jnp.int32, (TILE, TILE), 1)

    def attend(t):
        first, end = t * TILE, (t + 1) * TILE
        rounded = weights[t % len(weights)]
        q = qt[:, first:end]
        s = sublanes(jnp.where(down <= across, scores(first, q), -jnp.inf))
        shift = jnp.max(s, axis=0)
        shift = jnp.broadcast_to(jnp.max(shift, axis=0, keepdims=True), shift.shape)
        exponent = jnp.exp2((s - shift) * SCALE)
        total = jnp.sum(exponent, axis=0)
        rounded[first:end] = exponent.reshape(TILE, TILE).astype(jnp.bfloat16)
        for key in range(0, first, TILE):
            s = sublanes(scores(key, q))
            exponent = jnp.exp2((s - shift) * SCALE)
            total = total + jnp.sum(exponent, axis=0)
            rounded[key : key + TILE] = exponent.reshape(TILE, TILE).astype(jnp.bfloat16)
        summed = jnp.dot(vt[:, :end], rounded[:end], preferred_element_type=jnp.float32)
        total = jnp.sum(total, axis=0, keepdims=True)
        o_ref[first:end, :] = (summed / total).T.astype(jnp.bfloat16)
        return jnp.max(total)

    for s in range(3):
        held[s, :8] = jnp.zeros((8, HEAD_DIM), jnp.float32)
    largest = 0.0
    for first in range(0, length, STRETCH):
        featurize(first, STRETCH)
    for t in range(length // TILE):
        largest = jnp.maximum(largest, attend(t))

    @pl.when(jnp.logical_not(largest < HIGHEST_TOTAL))
    def _():
        def query_tile(t, _):
            first = pl.multiple_of(t * TILE, TILE)
            q = qt[:, pl.ds(first, TILE)]

            def key_tile(number, carry):
                m, l, acc = carry
                key = pl.multiple_of(number * TILE, TILE)
                s = jnp.where(key + down <= first + across, scores(key, q), -jnp.inf)
                new = jnp.maximum(m, jnp.max(s, axis=0, keepdims=True))
                alpha = jnp.exp2((m - new) * SCALE)
                exponent = jnp.exp2((s - new) * SCALE)
                l = l * alpha + jnp.sum(exponent, axis=0, keepdims=True)
                acc = acc * alpha + jnp.dot(
                    vt[:, pl.ds(key, TILE)],
                    exponent.astype(jnp.bfloat16),
                    preferred_element_type=jnp.float32,
                )
                return new, l, acc

            start = (
                jnp.full((1, TILE), -jnp.inf, jnp.float32),
                jnp.zeros((1, TILE), jnp.float32),
                jnp.zeros((HEAD_DIM, TILE), jnp.float32),
            )
            _, l, acc = lax.fori_loop(0, t + 1, key_tile, start)
            o_ref[pl.ds(first, TILE), :] = (acc / l).T.astype(jnp.bfloat16)
            return 0

        lax.fori_loop(0, length // TILE, query_tile, 0)


def attention(x, taps):
    shards, rows, _ = x.shape
    length = shards * rows // 3
    return pl.pallas_call(
        attention_kernel,
        out_shape=jax.ShapeDtypeStruct((length, HEAD_DIM), jnp.bfloat16),
        in_specs=[VMEM] * 2,
        out_specs=VMEM,
        scratch_shapes=[
            pltpu.VMEM((HEAD_DIM, length), jnp.bfloat16),
            pltpu.VMEM((length, HEAD_DIM), jnp.bfloat16),
            pltpu.VMEM((HEAD_DIM, length), jnp.bfloat16),
            pltpu.VMEM((3, 8 + length, HEAD_DIM), jnp.float32),
            pltpu.VMEM((length, TILE), jnp.bfloat16),
            pltpu.VMEM((length, TILE), jnp.bfloat16),
        ],
        compiler_params=pltpu.CompilerParams(vmem_limit_bytes=32 * 2**20),
        name="attention",
    )(x, taps)


def own_taps(filters):
    head = lax.axis_index("ctx")
    here = filters.shape[2] // HEAD_DIM
    mine = lax.dynamic_slice_in_dim(filters, (head % here) * HEAD_DIM, HEAD_DIM, axis=2)
    mine = jnp.where(head // here == lax.axis_index("fsdp"), mine, 0.0)
    return lax.psum(mine, "fsdp")


def exchanged(parts):
    return lax.all_to_all(parts, "ctx", split_axis=0, concat_axis=0, tiled=True)


def on_device(streams, filters):
    seqs_here, positions, channel_width = streams.shape
    taps = own_taps(filters)
    arrived = exchanged(split_by_head(streams.reshape(positions, channel_width)))
    attended = attention(arrived, taps)
    returned = exchanged(attended.reshape(HEADS, positions, HEAD_DIM))
    return merge_heads(returned).reshape(seqs_here, positions, HEADS * HEAD_DIM)


def solution(mesh):
    placed = (P("fsdp", "ctx", None), P(None, None, "fsdp"))
    return jax.shard_map(
        on_device, mesh=mesh, in_specs=placed, out_specs=P("fsdp", "ctx", None), check_vma=False
    )
```

```python
import functools
import math

import jax
import jax.numpy as jnp
from jax import lax
from jax.experimental import pallas as pl
from jax.experimental.pallas import tpu as pltpu
from jax.sharding import PartitionSpec as P

HEADS = 32
HEAD_DIM = 128
TAPS = 3
SCALE = HEAD_DIM**-0.5 * math.log2(math.e)
TILE = 256
HALF = TILE // 2
STRETCH = 1024
ROWS = 16
HEADS_AT_A_TIME = 8
HIGHEST_TOTAL = 2.0**60
VMEM = pl.BlockSpec(memory_space=pltpu.VMEM)


def split_kernel(x_ref, out_ref, rows, by_head, arrived, sent):
    positions, width = x_ref.shape
    step = HEADS_AT_A_TIME * HEAD_DIM

    def fetch(part):
        columns = pl.ds(part * step, step)
        return pltpu.make_async_copy(x_ref.at[:, columns], rows.at[:, columns], arrived.at[part])

    def send(part):
        stream, first = divmod(part * HEADS_AT_A_TIME, HEADS)
        heads, kept = pl.ds(first, HEADS_AT_A_TIME), pl.ds(stream * positions, positions)
        place = out_ref.at[heads, kept, :]
        return pltpu.make_async_copy(by_head.at[heads, kept, :], place, sent.at[part])

    for part in range(width // step):
        fetch(part).start()
    for part in range(width // step):
        fetch(part).wait()
        for column in range(part * HEADS_AT_A_TIME, (part + 1) * HEADS_AT_A_TIME):
            stream, head = divmod(column, HEADS)
            by_head[head, stream * positions : (stream + 1) * positions, :] = rows[
                :, column * HEAD_DIM : (column + 1) * HEAD_DIM
            ]
        send(part).start()
    for part in range(width // step):
        send(part).wait()


def split_by_head(streams):
    positions, width = streams.shape
    parts = 3 * HEADS // HEADS_AT_A_TIME
    shape = (HEADS, 3 * positions, HEAD_DIM)
    return pl.pallas_call(
        split_kernel,
        out_shape=jax.ShapeDtypeStruct(shape, jnp.bfloat16),
        in_specs=[pl.BlockSpec(memory_space=pltpu.HBM)],
        out_specs=pl.BlockSpec(memory_space=pltpu.HBM),
        scratch_shapes=[
            pltpu.VMEM((positions, width), jnp.bfloat16),
            pltpu.VMEM(shape, jnp.bfloat16),
            pltpu.SemaphoreType.DMA((parts,)),
            pltpu.SemaphoreType.DMA((parts,)),
        ],
        compiler_params=pltpu.CompilerParams(vmem_limit_bytes=58 * 2**20),
        name="split_by_head",
    )(streams)


def merge_kernel(in_ref, out_ref, rows, sent):
    heads, positions, _ = in_ref.shape
    count = positions // ROWS

    def copy(part):
        chunk = pl.ds(part * ROWS, ROWS)
        return pltpu.make_async_copy(rows.at[chunk, :], out_ref.at[chunk, :], sent.at[part])

    for part in range(count):
        first = part * ROWS
        for head in range(heads):
            rows[first : first + ROWS, head * HEAD_DIM : (head + 1) * HEAD_DIM] = in_ref[
                head, first : first + ROWS, :
            ]
        copy(part).start()
    for part in range(count):
        copy(part).wait()


def merge_heads(parts):
    heads, positions, _ = parts.shape
    return pl.pallas_call(
        merge_kernel,
        out_shape=jax.ShapeDtypeStruct((positions, heads * HEAD_DIM), jnp.bfloat16),
        in_specs=[VMEM],
        out_specs=pl.BlockSpec(memory_space=pltpu.HBM),
        scratch_shapes=[
            pltpu.VMEM((positions, heads * HEAD_DIM), jnp.bfloat16),
            pltpu.SemaphoreType.DMA((positions // ROWS,)),
        ],
        compiler_params=pltpu.CompilerParams(vmem_limit_bytes=16 * 2**20),
        name="merge_heads",
    )(parts)


def sublanes(x):
    return x.reshape(x.shape[0] // 8, 8, x.shape[1])


def attention_kernel(x_ref, taps_ref, o_ref, qt, kf, vt, held, *weights):
    shards, positions = x_ref.shape[0], x_ref.shape[1] // 3
    length = shards * positions
    taps = [[taps_ref[s, offset : offset + 1, :] for offset in range(TAPS)] for s in range(3)]

    def featurize(first, rows):
        for s in range(3):
            shard, after = first // positions, (first + rows) // positions
            x = x_ref[shard:after, s * positions : (s + 1) * positions, :]
            x = x.reshape(rows, HEAD_DIM).astype(jnp.float32)
            held[s, 8 + first : 8 + first + rows] = x
            summed = taps[s][0] * x
            for offset in range(1, TAPS):
                start = 8 - offset + first
                summed = summed + taps[s][offset] * held[s, start : start + rows]
            featured = summed.astype(jnp.bfloat16)
            if s == 1:
                kf[first : first + rows, :] = featured
            else:
                (qt if s == 0 else vt)[:, first : first + rows] = featured.T

    def scores(key, q, count=TILE):
        return jnp.dot(kf[pl.ds(key, count), :], q, preferred_element_type=jnp.float32)

    down = lax.broadcasted_iota(jnp.int32, (TILE, TILE), 0)
    across = lax.broadcasted_iota(jnp.int32, (TILE, TILE), 1)
    causal = down <= across

    def attend(t):
        first, end = t * TILE, (t + 1) * TILE
        rounded = weights[t % len(weights)]
        q = qt[:, first:end]
        early = sublanes(jnp.where(causal[:HALF], scores(first, q, HALF), -jnp.inf))
        late = scores(first + HALF, q[:, HALF:], HALF)
        late = sublanes(jnp.where(causal[:HALF, :HALF], late, -jnp.inf))
        shift = jnp.max(early, axis=0)
        raised = jnp.maximum(shift[:, HALF:], jnp.max(late, axis=0))
        shift = jnp.concatenate([shift[:, :HALF], raised], axis=1)
        shift = jnp.broadcast_to(jnp.max(shift, axis=0, keepdims=True), shift.shape)
        early = jnp.exp2((early - shift) * SCALE)
        late = jnp.exp2((late - shift[:, HALF:]) * SCALE)
        total = jnp.sum(early, axis=0)
        raised = total[:, HALF:] + jnp.sum(late, axis=0)
        total = jnp.concatenate([total[:, :HALF], raised], axis=1)
        middle = first + HALF
        rounded[first:middle] = early.reshape(HALF, TILE).astype(jnp.bfloat16)
        rounded[middle:end, :HALF] = jnp.zeros((HALF, HALF), jnp.bfloat16)
        rounded[middle:end, HALF:] = late.reshape(HALF, HALF).astype(jnp.bfloat16)
        for key in range(0, first, TILE):
            s = sublanes(scores(key, q))
            exponent = jnp.exp2((s - shift) * SCALE)
            total = total + jnp.sum(exponent, axis=0)
            rounded[key : key + TILE] = exponent.reshape(TILE, TILE).astype(jnp.bfloat16)
        summed = jnp.dot(vt[:, :end], rounded[:end], preferred_element_type=jnp.float32)
        total = jnp.sum(total, axis=0, keepdims=True)
        o_ref[first:end, :] = (summed / total).T.astype(jnp.bfloat16)
        return jnp.max(total)

    for s in range(3):
        held[s, :8] = jnp.zeros((8, HEAD_DIM), jnp.float32)
    largest = 0.0
    for first in range(0, length, STRETCH):
        featurize(first, STRETCH)
    for t in range(length // TILE):
        largest = jnp.maximum(largest, attend(t))

    @pl.when(jnp.logical_not(largest < HIGHEST_TOTAL))
    def _():
        def query_tile(t, _):
            first = pl.multiple_of(t * TILE, TILE)
            q = qt[:, pl.ds(first, TILE)]

            def key_tile(number, carry):
                m, l, acc = carry
                key = pl.multiple_of(number * TILE, TILE)
                s = jnp.where(key + down <= first + across, scores(key, q), -jnp.inf)
                new = jnp.maximum(m, jnp.max(s, axis=0, keepdims=True))
                alpha = jnp.exp2((m - new) * SCALE)
                exponent = jnp.exp2((s - new) * SCALE)
                l = l * alpha + jnp.sum(exponent, axis=0, keepdims=True)
                acc = acc * alpha + jnp.dot(
                    vt[:, pl.ds(key, TILE)],
                    exponent.astype(jnp.bfloat16),
                    preferred_element_type=jnp.float32,
                )
                return new, l, acc

            start = (
                jnp.full((1, TILE), -jnp.inf, jnp.float32),
                jnp.zeros((1, TILE), jnp.float32),
                jnp.zeros((HEAD_DIM, TILE), jnp.float32),
            )
            _, l, acc = lax.fori_loop(0, t + 1, key_tile, start)
            o_ref[pl.ds(first, TILE), :] = (acc / l).T.astype(jnp.bfloat16)
            return 0

        lax.fori_loop(0, length // TILE, query_tile, 0)


def attention(x, taps):
    shards, rows, _ = x.shape
    length = shards * rows // 3
    return pl.pallas_call(
        attention_kernel,
        out_shape=jax.ShapeDtypeStruct((length, HEAD_DIM), jnp.bfloat16),
        in_specs=[VMEM] * 2,
        out_specs=VMEM,
        scratch_shapes=[
            pltpu.VMEM((HEAD_DIM, length), jnp.bfloat16),
            pltpu.VMEM((length, HEAD_DIM), jnp.bfloat16),
            pltpu.VMEM((HEAD_DIM, length), jnp.bfloat16),
            pltpu.VMEM((3, 8 + length, HEAD_DIM), jnp.float32),
            pltpu.VMEM((length, TILE), jnp.bfloat16),
            pltpu.VMEM((length, TILE), jnp.bfloat16),
        ],
        compiler_params=pltpu.CompilerParams(vmem_limit_bytes=32 * 2**20),
        name="attention",
    )(x, taps)


def own_taps(filters):
    head = lax.axis_index("ctx")
    here = filters.shape[2] // HEAD_DIM
    mine = lax.dynamic_slice_in_dim(filters, (head % here) * HEAD_DIM, HEAD_DIM, axis=2)
    mine = jnp.where(head // here == lax.axis_index("fsdp"), mine, 0.0)
    return lax.psum(mine, "fsdp")


def exchanged(parts):
    return lax.all_to_all(parts, "ctx", split_axis=0, concat_axis=0, tiled=True)


def on_device(streams, filters):
    seqs_here, positions, channel_width = streams.shape
    taps = own_taps(filters)
    arrived = exchanged(split_by_head(streams.reshape(positions, channel_width)))
    attended = attention(arrived, taps)
    returned = exchanged(attended.reshape(HEADS, positions, HEAD_DIM))
    return merge_heads(returned).reshape(seqs_here, positions, HEADS * HEAD_DIM)


def solution(mesh):
    placed = (P("fsdp", "ctx", None), P(None, None, "fsdp"))
    return jax.shard_map(
        on_device, mesh=mesh, in_specs=placed, out_specs=P("fsdp", "ctx", None), check_vma=False
    )
```

```python
import functools
import math

import jax
import jax.numpy as jnp
from jax import lax
from jax.experimental import pallas as pl
from jax.experimental.pallas import tpu as pltpu
from jax.sharding import PartitionSpec as P

HEADS = 32
HEAD_DIM = 128
TAPS = 3
SCALE = HEAD_DIM**-0.5 * math.log2(math.e)
TILE = 256
HALF = TILE // 2
STRETCH = 1024
ROWS = 16
HEADS_AT_A_TIME = 8
HIGHEST_TOTAL = 2.0**60
VMEM = pl.BlockSpec(memory_space=pltpu.VMEM)


def split_kernel(x_ref, out_ref, rows, by_head, arrived, sent):
    positions, width = x_ref.shape
    step = HEADS_AT_A_TIME * HEAD_DIM

    def fetch(part):
        columns = pl.ds(part * step, step)
        return pltpu.make_async_copy(x_ref.at[:, columns], rows.at[:, columns], arrived.at[part])

    def send(part):
        stream, first = divmod(part * HEADS_AT_A_TIME, HEADS)
        heads, kept = pl.ds(first, HEADS_AT_A_TIME), pl.ds(stream * positions, positions)
        place = out_ref.at[heads, kept, :]
        return pltpu.make_async_copy(by_head.at[heads, kept, :], place, sent.at[part])

    for part in range(width // step):
        fetch(part).start()
    for part in range(width // step):
        fetch(part).wait()
        for column in range(part * HEADS_AT_A_TIME, (part + 1) * HEADS_AT_A_TIME):
            stream, head = divmod(column, HEADS)
            by_head[head, stream * positions : (stream + 1) * positions, :] = rows[
                :, column * HEAD_DIM : (column + 1) * HEAD_DIM
            ]
        send(part).start()
    for part in range(width // step):
        send(part).wait()


def split_by_head(streams):
    positions, width = streams.shape
    parts = 3 * HEADS // HEADS_AT_A_TIME
    shape = (HEADS, 3 * positions, HEAD_DIM)
    return pl.pallas_call(
        split_kernel,
        out_shape=jax.ShapeDtypeStruct(shape, jnp.bfloat16),
        in_specs=[pl.BlockSpec(memory_space=pltpu.HBM)],
        out_specs=pl.BlockSpec(memory_space=pltpu.HBM),
        scratch_shapes=[
            pltpu.VMEM((positions, width), jnp.bfloat16),
            pltpu.VMEM(shape, jnp.bfloat16),
            pltpu.SemaphoreType.DMA((parts,)),
            pltpu.SemaphoreType.DMA((parts,)),
        ],
        compiler_params=pltpu.CompilerParams(vmem_limit_bytes=58 * 2**20),
        name="split_by_head",
    )(streams)


def merge_kernel(in_ref, out_ref, rows, sent):
    heads, positions, _ = in_ref.shape
    count = positions // ROWS

    def copy(part):
        chunk = pl.ds(part * ROWS, ROWS)
        return pltpu.make_async_copy(rows.at[chunk, :], out_ref.at[chunk, :], sent.at[part])

    for part in range(count):
        first = part * ROWS
        for head in range(heads):
            rows[first : first + ROWS, head * HEAD_DIM : (head + 1) * HEAD_DIM] = in_ref[
                head, first : first + ROWS, :
            ]
        copy(part).start()
    for part in range(count):
        copy(part).wait()


def merge_heads(parts):
    heads, positions, _ = parts.shape
    return pl.pallas_call(
        merge_kernel,
        out_shape=jax.ShapeDtypeStruct((positions, heads * HEAD_DIM), jnp.bfloat16),
        in_specs=[VMEM],
        out_specs=pl.BlockSpec(memory_space=pltpu.HBM),
        scratch_shapes=[
            pltpu.VMEM((positions, heads * HEAD_DIM), jnp.bfloat16),
            pltpu.SemaphoreType.DMA((positions // ROWS,)),
        ],
        compiler_params=pltpu.CompilerParams(vmem_limit_bytes=16 * 2**20),
        name="merge_heads",
    )(parts)


def sublanes(x):
    return x.reshape(x.shape[0] // 8, 8, x.shape[1])


def attention_kernel(x_ref, taps_ref, o_ref, qt, kf, vt, held, *weights):
    shards, positions = x_ref.shape[0], x_ref.shape[1] // 3
    length = shards * positions
    taps = [[taps_ref[s, offset : offset + 1, :] for offset in range(TAPS)] for s in range(3)]

    def featurize(first, rows):
        for s in range(3):
            shard, after = first // positions, (first + rows) // positions
            x = x_ref[shard:after, s * positions : (s + 1) * positions, :]
            x = x.reshape(rows, HEAD_DIM).astype(jnp.float32)
            held[s, 8 + first : 8 + first + rows] = x
            summed = taps[s][0] * x
            for offset in range(1, TAPS):
                start = 8 - offset + first
                summed = summed + taps[s][offset] * held[s, start : start + rows]
            featured = summed.astype(jnp.bfloat16)
            if s == 1:
                kf[first : first + rows, :] = featured
            else:
                (qt if s == 0 else vt)[:, first : first + rows] = featured.T

    def scores(key, q, count=TILE):
        return jnp.dot(kf[pl.ds(key, count), :], q, preferred_element_type=jnp.float32)

    down = lax.broadcasted_iota(jnp.int32, (TILE, TILE), 0)
    across = lax.broadcasted_iota(jnp.int32, (TILE, TILE), 1)
    causal = down <= across

    def attend(t):
        first, end = t * TILE, (t + 1) * TILE
        rounded = weights[t % len(weights)]
        q = qt[:, first:end]
        early = sublanes(jnp.where(causal[:HALF], scores(first, q, HALF), -jnp.inf))
        late = scores(first + HALF, q[:, HALF:], HALF)
        late = sublanes(jnp.where(causal[:HALF, :HALF], late, -jnp.inf))
        shift = jnp.max(early, axis=0)
        raised = jnp.maximum(shift[:, HALF:], jnp.max(late, axis=0))
        shift = jnp.concatenate([shift[:, :HALF], raised], axis=1)
        shift = jnp.broadcast_to(jnp.max(shift, axis=0, keepdims=True), shift.shape)
        early = jnp.exp2((early - shift) * SCALE)
        late = jnp.exp2((late - shift[:, HALF:]) * SCALE)
        total = jnp.sum(early, axis=0)
        raised = total[:, HALF:] + jnp.sum(late, axis=0)
        total = jnp.concatenate([total[:, :HALF], raised], axis=1)
        middle = first + HALF
        rounded[first:middle] = early.reshape(HALF, TILE).astype(jnp.bfloat16)
        rounded[middle:end, :HALF] = jnp.zeros((HALF, HALF), jnp.bfloat16)
        rounded[middle:end, HALF:] = late.reshape(HALF, HALF).astype(jnp.bfloat16)
        for key in range(0, first, TILE):
            s = sublanes(scores(key, q))
            exponent = jnp.exp2((s - shift) * SCALE)
            total = total + jnp.sum(exponent, axis=0)
            rounded[key : key + TILE] = exponent.reshape(TILE, TILE).astype(jnp.bfloat16)
        summed = jnp.dot(vt[:, :end], rounded[:end], preferred_element_type=jnp.float32)
        total = jnp.sum(total, axis=0, keepdims=True)
        o_ref[first:end, :] = (summed / total).T.astype(jnp.bfloat16)
        return jnp.max(total)

    for s in range(3):
        held[s, :8] = jnp.zeros((8, HEAD_DIM), jnp.float32)
    largest = 0.0
    for first in range(0, length, STRETCH):
        featurize(first, STRETCH)
    for t in reversed(range(length // TILE)):
        largest = jnp.maximum(largest, attend(t))

    @pl.when(jnp.logical_not(largest < HIGHEST_TOTAL))
    def _():
        def query_tile(t, _):
            first = pl.multiple_of(t * TILE, TILE)
            q = qt[:, pl.ds(first, TILE)]

            def key_tile(number, carry):
                m, l, acc = carry
                key = pl.multiple_of(number * TILE, TILE)
                s = jnp.where(key + down <= first + across, scores(key, q), -jnp.inf)
                new = jnp.maximum(m, jnp.max(s, axis=0, keepdims=True))
                alpha = jnp.exp2((m - new) * SCALE)
                exponent = jnp.exp2((s - new) * SCALE)
                l = l * alpha + jnp.sum(exponent, axis=0, keepdims=True)
                acc = acc * alpha + jnp.dot(
                    vt[:, pl.ds(key, TILE)],
                    exponent.astype(jnp.bfloat16),
                    preferred_element_type=jnp.float32,
                )
                return new, l, acc

            start = (
                jnp.full((1, TILE), -jnp.inf, jnp.float32),
                jnp.zeros((1, TILE), jnp.float32),
                jnp.zeros((HEAD_DIM, TILE), jnp.float32),
            )
            _, l, acc = lax.fori_loop(0, t + 1, key_tile, start)
            o_ref[pl.ds(first, TILE), :] = (acc / l).T.astype(jnp.bfloat16)
            return 0

        lax.fori_loop(0, length // TILE, query_tile, 0)


def attention(x, taps):
    shards, rows, _ = x.shape
    length = shards * rows // 3
    return pl.pallas_call(
        attention_kernel,
        out_shape=jax.ShapeDtypeStruct((length, HEAD_DIM), jnp.bfloat16),
        in_specs=[VMEM] * 2,
        out_specs=VMEM,
        scratch_shapes=[
            pltpu.VMEM((HEAD_DIM, length), jnp.bfloat16),
            pltpu.VMEM((length, HEAD_DIM), jnp.bfloat16),
            pltpu.VMEM((HEAD_DIM, length), jnp.bfloat16),
            pltpu.VMEM((3, 8 + length, HEAD_DIM), jnp.float32),
            pltpu.VMEM((length, TILE), jnp.bfloat16),
            pltpu.VMEM((length, TILE), jnp.bfloat16),
        ],
        compiler_params=pltpu.CompilerParams(vmem_limit_bytes=32 * 2**20),
        name="attention",
    )(x, taps)


def own_taps(filters):
    head = lax.axis_index("ctx")
    here = filters.shape[2] // HEAD_DIM
    mine = lax.dynamic_slice_in_dim(filters, (head % here) * HEAD_DIM, HEAD_DIM, axis=2)
    mine = jnp.where(head // here == lax.axis_index("fsdp"), mine, 0.0)
    return lax.psum(mine, "fsdp")


def exchanged(parts):
    return lax.all_to_all(parts, "ctx", split_axis=0, concat_axis=0, tiled=True)


def on_device(streams, filters):
    seqs_here, positions, channel_width = streams.shape
    taps = own_taps(filters)
    arrived = exchanged(split_by_head(streams.reshape(positions, channel_width)))
    attended = attention(arrived, taps)
    returned = exchanged(attended.reshape(HEADS, positions, HEAD_DIM))
    return merge_heads(returned).reshape(seqs_here, positions, HEADS * HEAD_DIM)


def solution(mesh):
    placed = (P("fsdp", "ctx", None), P(None, None, "fsdp"))
    return jax.shard_map(
        on_device, mesh=mesh, in_specs=placed, out_specs=P("fsdp", "ctx", None), check_vma=False
    )
```
